256 devices in a mesh: wave: 32 (over x, z), field: 8 (over y, core).
Axes of the slice: x: 4, y: 4, z: 8, core: 2. Of those that a mesh axis runs over, the one named last changes fastest.
Arguments:
- spectral: bfloat16 [512, 2, 2, 48, 1025], P(('wave', 'field')), may hold values from -6 to 6
- legendre: bfloat16 [512, 1025, 1280], P(('wave', 'field')), may hold values from -0.1875 to 0.1875
- slot_pairs: int32 [512], replicated, may hold values from 0 to 511, each once
Outputs:
- grid_values: bfloat16 [48, 2560, 5120], P(None, 'wave', 'field')
The draws below stay inside these ranges and needn't reach their ends.
Inputs may be any that keep to these rules, and one draw needn't show every extreme that they name: `slot_pairs`: every pair 0 to 511 stands in exactly one slot.
All inputs are finite; a program needn't handle non-finite values.
Results may differ from the reference program's by a relative error of at most 0.0058.
Values may be sent and summed in bfloat16 or wider, within the bound.
A program may use at most 128 MiB of HBM per device.

```python
import math
import jax
import jax.numpy as jnp
from jax import lax

M = 1024
NLAT = 2560
NLON = 5120
FLEV = 48
PAIRS = 512


def block_scale(rng, extent, split, least, largest):
    level = 1.0
    for dim, parts in split:
        steps = jax.random.uniform(jax.random.fold_in(jax.random.fold_in(rng, 6), dim), (parts,), jnp.float32, least / len(split), largest / len(split))
        level = level * jnp.repeat(jnp.exp(steps), extent[dim] // parts).reshape((-1,) + (1,) * (len(extent) - 1 - dim))
    return level


def normal_values(key, shape, width, most, pieces=(), kind=jnp.bfloat16):
    entries = jax.random.normal(key, shape, jnp.float32) * width
    if len(pieces) > 0:
        entries = block_scale(key, shape, pieces, -0.22, 0.18) * entries
    return jnp.clip(entries, min=-most, max=most).astype(kind)


def setup_inputs(seed: int = 0) -> dict:
    arg_keys = jax.random.split(jax.random.key(seed), 4)
    return {
        "spectral": normal_values(arg_keys[0], (PAIRS, 2, 2, FLEV, M + 1), 1.0, 6.0, ((0, 256),)),
        "legendre": normal_values(arg_keys[1], (PAIRS, M + 1, NLAT // 2), M ** -0.5, 0.1875, ((0, 256),)),
        "slot_pairs": jax.random.permutation(arg_keys[2], PAIRS).astype(jnp.int32),
    }


def row_masks(pair_ids, degree_top):
    row_index = jnp.arange(degree_top + 1, dtype=jnp.int32)
    boundary = (degree_top - pair_ids)[:, None]
    first_half = row_index[None, :] < boundary
    distance = jnp.where(first_half, row_index[None, :], row_index[None, :] - boundary)
    even_rows = distance % 2 == 0
    owners = jnp.stack([first_half, jnp.logical_not(first_half)], axis=1)
    parity = jnp.stack([even_rows, jnp.logical_not(even_rows)], axis=1)
    return jnp.logical_and(parity[:, :, None, :], owners[:, None, :, :])

def masked_terms(spectral, pair_ids, degree_top):
    selector = row_masks(pair_ids, degree_top)
    zero_value = jnp.zeros((), jnp.bfloat16)
    return jnp.where(selector[:, :, :, None, None, :], spectral[:, None], zero_value)

def hemispheres(legendre_sums):
    even_part = legendre_sums[:, 0]
    odd_part = legendre_sums[:, 1]
    northern = even_part + odd_part
    southern = jnp.flip(even_part - odd_part, axis=-1)
    return jnp.concatenate([northern, southern], axis=-1).astype(jnp.bfloat16)

def wave_numbers(pair_ids):
    return jnp.stack([pair_ids, M - 1 - pair_ids], axis=1).reshape(pair_ids.shape[0] * 2)

def wave_table(numbers, longitudes):
    phase_index = numbers[:, None] * longitudes[None, :] % NLON
    angles = phase_index.astype(jnp.float32) * (2.0 * math.pi / NLON)
    weight = jnp.where(numbers == 0, 1.0 / math.sqrt(2.0 * M), 2.0 / math.sqrt(2.0 * M)).astype(jnp.float32)
    cosine = weight[:, None] * jnp.cos(angles)
    sine_part = -weight[:, None] * jnp.sin(angles)
    stacked = jnp.stack([cosine, sine_part], axis=1)
    return stacked.reshape(numbers.shape[0] * 2, longitudes.shape[0]).astype(jnp.bfloat16)

def reference(spectral, legendre, slot_pairs):
    pair_ids = slot_pairs.astype(jnp.int32)
    field_levels = spectral.shape[3]

    def one_slot(operands):
        coeffs, table_slot, pair_one = operands
        masked = masked_terms(coeffs[None], pair_one[None], M)[0]
        legendre_sums = jnp.dot(masked.reshape(8 * field_levels, M + 1), table_slot, preferred_element_type=jnp.float32)
        return hemispheres(legendre_sums.reshape(1, 2, 2, 2, field_levels, NLAT // 2))[0]
    fourier = lax.map(one_slot, (spectral, legendre, pair_ids))
    basis_rows = wave_table(wave_numbers(pair_ids), jnp.arange(NLON, dtype=jnp.int32))
    stacked = jnp.moveaxis(fourier, 3, 0).reshape(field_levels, PAIRS * 4, NLAT)

    def one_level(level_block):
        return jnp.dot(level_block.T, basis_rows, preferred_element_type=jnp.float32).astype(jnp.bfloat16)
    return lax.map(one_level, stacked)
```

```python
import functools
import math

import jax
import jax.numpy as jnp
from jax import lax
from jax.experimental import pallas as pl
from jax.experimental.pallas import tpu as pltpu
from jax.sharding import PartitionSpec as P

M = 1024
NLON = 5120
NORTH = 1280
FLEV = 48
XS, ZS, YS = 4, 8, 4
WAVES = XS * ZS
FIELDS = 2 * YS
BAND = 80
LONS = 640
PIECE = 16
PIECES = BAND // PIECE
LANES = 8 * FLEV
DEPTH = 8 * WAVES
MESH = pl.DeviceIdType.MESH
F32 = jnp.float32
BF16 = jnp.bfloat16


def iota(shape, dim):
    return lax.broadcasted_iota(jnp.int32, shape, dim)


def one_hot(condition):
    return jnp.where(condition, 1.0, 0.0).astype(BF16)


def legendre_kernel(pairs_ref, spectral_ref, legendre_ref, send_ref, sums):
    slot = pl.program_id(0)
    pair = pairs_ref[slot]
    rows = M + 1
    boundary = M - pair
    row = iota((2 * FLEV, rows), 1)
    in_first = row < boundary
    distance = jnp.where(in_first, row, row - boundary)
    sign = jnp.where(distance % 2 == 0, 1.0, -1.0)
    first = spectral_ref[0, : 2 * FLEV, :].astype(F32)
    second = spectral_ref[0, 2 * FLEV :, :].astype(F32)
    first = jnp.where(in_first, first, 0.0)
    second = jnp.where(in_first, 0.0, second)
    terms = jnp.concatenate([first, second, first * sign, second * sign], axis=0).astype(BF16)
    sums[slot] = jnp.dot(terms, legendre_ref[0], preferred_element_type=F32).astype(BF16)

    @pl.when(slot == 1)
    def _():
        half = 4 * FLEV
        target = iota((LANES, LANES), 0)
        source = target % 8 // 4 * half + target % 4 * FLEV + target // 8
        order = one_hot(iota((LANES, LANES), 1) == source)
        lat = iota((BAND, 256), 0)
        col = iota((BAND, 256), 1)
        for south in range(2):
            stacked = jnp.concatenate(
                [sums[k, south * half : (south + 1) * half, :] for k in range(2)], axis=0
            )
            ordered = jnp.dot(order, stacked, preferred_element_type=F32).astype(BF16)
            for band in range(NORTH // BAND):
                start = min(band * BAND // 128 * 128, NORTH - 256)
                offset = band * BAND - start
                pick = one_hot(col == (offset + BAND - 1 - lat if south else offset + lat))
                chunk = lax.dot_general(
                    pick,
                    ordered[:, start : start + 256],
                    (((1,), (1,)), ((), ())),
                    preferred_element_type=F32,
                )
                send_ref[WAVES - 1 - band if south else band] = chunk.astype(BF16)


def legendre_stage(own_pairs, spectral, legendre):
    return pl.pallas_call(
        legendre_kernel,
        grid=(2,),
        out_shape=jax.ShapeDtypeStruct((WAVES, BAND, LANES), BF16),
        in_specs=[
            pl.BlockSpec(memory_space=pltpu.SMEM),
            pl.BlockSpec((1, 4 * FLEV, M + 1), lambda k: (k, 0, 0)),
            pl.BlockSpec((1, M + 1, NORTH), lambda k: (k, 0, 0)),
        ],
        out_specs=pl.BlockSpec((WAVES, BAND, LANES), lambda k: (0, 0, 0)),
        scratch_shapes=[pltpu.VMEM((2, 8 * FLEV, NORTH), BF16)],
        compiler_params=pltpu.CompilerParams(vmem_limit_bytes=40 << 20),
        name="legendre",
    )(own_pairs, spectral, legendre)


COS = [(-1.0) ** k * (2.0 * math.pi) ** (2 * k) / math.factorial(2 * k) for k in range(12)]


def grid_kernel(
    send_ref, number_ref, out_ref,
    landed, whole, basis, swap_outer, swap_inner, result,
    a2a_send, a2a_recv, y_send, y_recv, fwd_send, fwd_recv, core_send, core_recv, out_sem,
):
    wave = lax.axis_index("wave")
    field = lax.axis_index("field")
    x, z = wave // ZS, wave % ZS
    y, core = field // 2, field % 2
    up = lax.rem(y + 1, YS) * 2 + core
    down = lax.rem(y + YS - 1, YS) * 2 + core
    across = lax.rem(y + 2, YS) * 2 + core
    other = 1 - core
    mate = y * 2 + other

    def peer_of(i):
        return lax.rem(x + i // ZS, XS) * ZS + lax.rem(z + i % ZS, ZS)

    barrier = pltpu.get_barrier_semaphore()
    for there in (up, down, mate):
        pl.semaphore_signal(barrier, inc=1, device_id=(wave, there), device_id_type=MESH)

    def greet(i, carry):
        pl.semaphore_signal(barrier, inc=1, device_id=(peer_of(i), field), device_id_type=MESH)
        return carry

    lax.fori_loop(1, WAVES, greet, 0)
    pl.semaphore_wait(barrier, WAVES + 2)

    def scatter(p):
        def one(i, carry):
            peer = peer_of(i)
            pltpu.make_async_remote_copy(
                src_ref=send_ref.at[peer, pl.ds(p * PIECE, PIECE), :],
                dst_ref=landed.at[p, wave],
                send_sem=a2a_send.at[p],
                recv_sem=a2a_recv.at[p],
                device_id=(peer, field),
                device_id_type=MESH,
            ).start()
            return carry

        lax.fori_loop(1, WAVES, one, 0)
        landed[p, wave] = send_ref[wave, p * PIECE : (p + 1) * PIECE, :]

    def wait_all(p, sem):
        block = landed.at[p, pl.ds(0, WAVES - 1)]
        pltpu.make_async_copy(block, block, sem.at[p]).wait()

    half = FLEV // 2

    def remote(p, source, part, send, recv, slot, there):
        lo, size = ((0, FLEV), (0, half), (half, half))[part]
        block = whole.at[p, source, pl.ds(lo, size)]
        return pltpu.make_async_remote_copy(
            src_ref=block, dst_ref=block, send_sem=send.at[p, slot], recv_sem=recv.at[p, slot],
            device_id=(wave, there), device_id_type=MESH,
        )

    def to_up(p):
        return remote(p, field, 0, y_send, y_recv, 0, up)

    def to_down(p):
        return remote(p, field, 0, y_send, y_recv, 1, down)

    def fwd_up(p):
        return remote(p, down, 1, fwd_send, fwd_recv, 0, up)

    def fwd_down(p):
        return remote(p, up, 2, fwd_send, fwd_recv, 1, down)

    def to_mate(p, k):
        source, part = ((field, 0), (down, 0), (up, 0), (across, 1), (across, 2))[k]
        return remote(p, source, part, core_send, core_recv, k, mate)

    def from_mate(p, k):
        yy = lambda s: s // 2 * 2 + other
        source, part = ((yy(field), 0), (yy(down), 0), (yy(up), 0), (yy(across), 1), (yy(across), 2))[k]
        return remote(p, source, part, core_send, core_recv, k, mate)

    def from_down(p):
        return remote(p, down, 0, y_send, y_recv, 0, down)

    def from_up(p):
        return remote(p, up, 0, y_send, y_recv, 1, up)

    def half_from_down(p):
        return remote(p, across, 1, fwd_send, fwd_recv, 0, down)

    def half_from_up(p):
        return remote(p, across, 2, fwd_send, fwd_recv, 1, up)

    def gather(p):
        wait_all(p, a2a_recv)
        got = landed[p].reshape(2, 4, 4, PIECE, LANES)
        groups = LANES // 128
        rows = groups * 8 * PIECE
        lhs = jnp.concatenate(
            [
                jnp.concatenate(
                    [
                        got[:, s1, :, :, 128 * g : 128 * (g + 1)].reshape(8 * PIECE, 128)
                        for g in range(groups)
                    ],
                    axis=0,
                )
                for s1 in range(4)
            ],
            axis=1,
        )
        mixed = jnp.dot(lhs, swap_outer[...], preferred_element_type=F32).astype(BF16)
        mixed = mixed.reshape(groups * 2, 4, PIECE, 512)
        lhs = jnp.concatenate(
            [
                jnp.concatenate(
                    [
                        mixed[:, s0, :, 128 * f1 : 128 * (f1 + 1)].reshape(groups * 2 * PIECE, 128)
                        for f1 in range(4)
                    ],
                    axis=0,
                )
                for s0 in range(4)
            ],
            axis=1,
        )
        done = jnp.dot(lhs, swap_inner[...], preferred_element_type=F32).astype(BF16)
        done = done.reshape(4, groups, 2, PIECE, 512)
        for f1 in range(4):
            for g in range(groups):
                for f0 in range(4):
                    for s in range(2):
                        whole[p, field, g * 16 + f1 * 4 + f0, :, 128 * s : 128 * (s + 1)] = done[
                            f1, g, s, :, 128 * f0 : 128 * (f0 + 1)
                        ]
        to_up(p).start()
        to_down(p).start()
        to_mate(p, 0).start()

    def relay(p):
        from_down(p).wait_recv()
        fwd_up(p).start()
        to_mate(p, 1).start()
        from_up(p).wait_recv()
        fwd_down(p).start()
        to_mate(p, 2).start()

    def finish(p):
        half_from_down(p).wait_recv()
        to_mate(p, 3).start()
        half_from_up(p).wait_recv()
        to_mate(p, 4).start()

    def out_copy(p, slot):
        return pltpu.make_async_copy(
            result.at[slot], out_ref.at[:, pl.ds(p * PIECE, PIECE), :], out_sem.at[slot]
        )

    def synthesize(p):
        for k in range(5):
            from_mate(p, k).wait_recv()
        slot = p % 2
        if p >= 2:
            out_copy(p - 2, slot).wait()
        levels = 12

        def block(i, carry):
            at = pl.ds(pl.multiple_of(i * levels, levels), levels)
            lhs = jnp.concatenate(
                [whole[p, s, at].reshape(levels * PIECE, DEPTH) for s in range(FIELDS)], axis=1
            )
            summed = jnp.dot(lhs, basis[...], preferred_element_type=F32)
            result[slot, at] = summed.astype(BF16).reshape(levels, PIECE, LONS)
            return carry

        lax.fori_loop(0, FLEV // levels, block, 0)
        out_copy(p, slot).start()

    scatter(0)
    scatter(1)

    a, b = iota((512, 512), 0), iota((512, 512), 1)
    swap_outer[...] = one_hot(b == a // 32 % 4 * 128 + a // 128 * 32 + a % 32)
    swap_inner[...] = one_hot(b == a // 8 % 4 * 128 + a // 32 % 4 * 32 + a // 128 * 8 + a % 8)

    def basis_block(i, carry):
        size = 128
        at = pl.ds(pl.multiple_of(i * size, size), size)
        number = number_ref[at, :]
        part = (iota((size, 1), 0) % 2).astype(F32)
        weight = jnp.where(number == 0.0, 1.0 / math.sqrt(2.0 * M), 2.0 / math.sqrt(2.0 * M))
        longitude = (field * LONS + iota((size, LONS), 1)).astype(F32)
        phase = number * longitude + part * (NLON // 4)
        phase = phase - NLON * jnp.floor(phase * (1.0 / NLON) + 0.5)
        turn = phase * (1.0 / NLON)
        square = turn * turn
        value = COS[-1]
        for c in COS[-2::-1]:
            value = value * square + c
        basis[at, :] = (weight * value).astype(BF16)
        return carry

    lax.fori_loop(0, DEPTH * FIELDS // 128, basis_block, 0)

    for t in range(PIECES + 3):
        if t < PIECES:
            gather(t)
            if t + 2 < PIECES:
                scatter(t + 2)
        if 0 <= t - 1 < PIECES:
            relay(t - 1)
        if 0 <= t - 2 < PIECES:
            finish(t - 2)
        if 0 <= t - 3 < PIECES:
            synthesize(t - 3)

    for p in range(PIECES):
        wait_all(p, a2a_send)
        to_up(p).wait_send()
        to_down(p).wait_send()
        fwd_up(p).wait_send()
        fwd_down(p).wait_send()
        for k in range(5):
            to_mate(p, k).wait_send()
    out_copy(PIECES - 2, (PIECES - 2) % 2).wait()
    out_copy(PIECES - 1, (PIECES - 1) % 2).wait()


def grid_stage(send, numbers):
    dma = pltpu.SemaphoreType.DMA
    return pl.pallas_call(
        grid_kernel,
        out_shape=jax.ShapeDtypeStruct((FLEV, BAND, LONS), BF16),
        in_specs=[pl.BlockSpec(memory_space=pltpu.VMEM)] * 2,
        out_specs=pl.BlockSpec(memory_space=pl.ANY),
        scratch_shapes=[
            pltpu.VMEM((PIECES, WAVES, PIECE, LANES), BF16),
            pltpu.VMEM((PIECES, FIELDS, FLEV, PIECE, DEPTH), BF16),
            pltpu.VMEM((DEPTH * FIELDS, LONS), BF16),
            pltpu.VMEM((512, 512), BF16),
            pltpu.VMEM((512, 512), BF16),
            pltpu.VMEM((2, FLEV, PIECE, LONS), BF16),
            dma((PIECES,)), dma((PIECES,)),
            dma((PIECES, 2)), dma((PIECES, 2)),
            dma((PIECES, 2)), dma((PIECES, 2)),
            dma((PIECES, 5)), dma((PIECES, 5)),
            dma((2,)),
        ],
        compiler_params=pltpu.CompilerParams(
            collective_id=0, has_side_effects=True, vmem_limit_bytes=56 << 20
        ),
        name="grid",
    )(send, numbers)


def shards(spectral, legendre, slot_pairs):
    per_device = spectral.shape[0]
    start_slot = lax.axis_index(("wave", "field")) * per_device
    own_pairs = lax.dynamic_slice_in_dim(slot_pairs, start_slot, per_device)
    send = legendre_stage(own_pairs, spectral.reshape(per_device, 4 * FLEV, M + 1), legendre)
    pairs = slot_pairs.reshape(WAVES, FIELDS, per_device).transpose(1, 0, 2).reshape(-1)
    numbers = jnp.stack([pairs, M - 1 - pairs], axis=1).reshape(-1, 1)
    numbers = jnp.repeat(numbers, 2, axis=0)
    return grid_stage(send, numbers.astype(F32))


def solution(mesh):
    in_specs = (P(("wave", "field"), None, None, None, None), P(("wave", "field"), None, None), P())
    out_specs = P(None, "wave", "field")
    return jax.shard_map(shards, mesh=mesh, in_specs=in_specs, out_specs=out_specs, check_vma=False)
```

```python
import math

import jax
import jax.numpy as jnp
from jax import lax
from jax.experimental import pallas as pl
from jax.experimental.pallas import tpu as pltpu
from jax.sharding import PartitionSpec as P

M = 1024
PAIRS = 512
NLON = 5120
NORTH = 1280
FLEV = 48
XS, ZS, YS = 4, 8, 4
WAVES = XS * ZS
FIELDS = 2 * YS
BAND = 80
LONS = 640
TILE = 16
PIECES = BAND // TILE
GROUPS = FLEV // TILE
STEPS = PIECES * GROUPS
HALF = 4 * FLEV
LANES = 8 * FLEV
DEPTH = 8 * WAVES
LAG_RELAY, LAG_FINISH, LAG_GRID = 2, 3, 4
BASIS_FROM, BASIS_STEPS = 3, 4
CAUGHT_UP = 2 * (BASIS_FROM + BASIS_STEPS) - LAG_GRID
MESH = pl.DeviceIdType.MESH
F32 = jnp.float32
BF16 = jnp.bfloat16
SINE = [(-1.0) ** k * (2.0 * math.pi) ** (2 * k + 1) / math.factorial(2 * k + 1) for k in range(8)]


def iota(shape, dim):
    return lax.broadcasted_iota(jnp.int32, shape, dim)


def one_hot(condition):
    return jnp.where(condition, 1.0, 0.0).astype(BF16)


def matmul(a, b):
    return jnp.dot(a, b, preferred_element_type=F32)


def kernel(
    pairs_ref, sums_ref, out_ref,
    send, landed, whole, basis, swap_outer, swap_inner,
    a2a_send, a2a_recv, y_send, y_recv, fwd_send, fwd_recv, core_send, core_recv,
):
    wave = lax.axis_index("wave")
    field = lax.axis_index("field")
    x, z = wave // ZS, wave % ZS
    y, core = field // 2, field % 2
    up = lax.rem(y + 1, YS) * 2 + core
    down = lax.rem(y + YS - 1, YS) * 2 + core
    across = lax.rem(y + 2, YS) * 2 + core
    other = 1 - core
    mate = y * 2 + other

    def peer_of(i):
        return lax.rem(x + i // ZS, XS) * ZS + lax.rem(z + i % ZS, ZS)

    barrier = pltpu.get_barrier_semaphore()
    for there in (up, down, mate):
        pl.semaphore_signal(barrier, inc=1, device_id=(wave, there), device_id_type=MESH)

    def greet(i, carry):
        pl.semaphore_signal(barrier, inc=1, device_id=(peer_of(i), field), device_id_type=MESH)
        return carry

    lax.fori_loop(1, WAVES, greet, 0)

    def turn(g):
        a, b = iota((256, 256), 0), iota((256, 256), 1)
        for south in range(2):
            pick = one_hot(a + b == 255 if south else a == b)
            for u in range(NORTH // 256):
                start = NORTH - 256 * (u + 1) if south else 256 * u
                rows = [
                    sums_ref[k, lo : lo + TILE, start : start + 256]
                    for k in range(2)
                    for lo in range(south * HALF + g * TILE, (south + 1) * HALF, FLEV)
                ]
                turned = lax.dot_general(
                    pick,
                    jnp.concatenate(rows, axis=0),
                    (((1,), (1,)), ((), ())),
                    preferred_element_type=F32,
                )
                at = south * NORTH // TILE + u * 16
                send[at : at + 16, :, g * 128 : (g + 1) * 128] = turned.astype(BF16).reshape(
                    16, TILE, 128
                )

    def scatter(p, lane, lanes, sem):
        def one(i, carry):
            peer = peer_of(i)
            pltpu.make_async_remote_copy(
                src_ref=send.at[peer * PIECES + p, :, pl.ds(lane, lanes)],
                dst_ref=landed.at[p, wave, :, pl.ds(lane, lanes)],
                send_sem=a2a_send.at[sem],
                recv_sem=a2a_recv.at[sem],
                device_id=(peer, field),
                device_id_type=MESH,
            ).start()
            return carry

        lax.fori_loop(1, WAVES, one, 0)

    def wait_all(p, lane, lanes, sem):
        block = landed.at[p, pl.ds(0, WAVES - 1), :, pl.ds(lane, lanes)]
        pltpu.make_async_copy(block, block, sem).wait()

    def remote(t, source, part, send_sem, recv_sem, slot, there):
        lo, size = ((0, TILE), (0, TILE // 2), (TILE // 2, TILE // 2))[part]
        block = whole.at[t, source, pl.ds(lo, size)]
        return pltpu.make_async_remote_copy(
            src_ref=block, dst_ref=block,
            send_sem=send_sem.at[t, slot], recv_sem=recv_sem.at[t, slot],
            device_id=(wave, there), device_id_type=MESH,
        )

    def to_up(t, source=field):
        return remote(t, source, 0, y_send, y_recv, 0, up)

    def to_down(t, source=field):
        return remote(t, source, 0, y_send, y_recv, 1, down)

    def fwd_up(t, source=down):
        return remote(t, source, 1, fwd_send, fwd_recv, 0, up)

    def fwd_down(t, source=up):
        return remote(t, source, 2, fwd_send, fwd_recv, 1, down)

    def to_mate(t, k, flip=0):
        source, part = ((field, 0), (down, 0), (up, 0), (across, 1), (across, 2))[k]
        if flip:
            source = source // 2 * 2 + other
        return remote(t, source, part, core_send, core_recv, k, mate)

    def gather(t):
        p, g = t // GROUPS, lax.rem(t, GROUPS)

        @pl.when(p == 0)
        def _():
            wait_all(0, pl.multiple_of(g * 128, 128), 128, a2a_recv.at[g])

        @pl.when(jnp.logical_and(p > 0, g == 0))
        def _():
            wait_all(p, 0, LANES, a2a_recv.at[GROUPS - 1 + p])

        got = landed[p, :, :, pl.ds(pl.multiple_of(g * 128, 128), 128)]
        got = got.reshape(2, 4, 4, TILE, 128)
        lhs = jnp.concatenate([got[:, s1].reshape(128, 128) for s1 in range(4)], axis=1)
        mixed = matmul(lhs, swap_outer[...]).astype(BF16).reshape(2, 4, TILE, 512)
        lhs = jnp.concatenate(
            [
                jnp.concatenate(
                    [
                        mixed[:, s0, :, 128 * f1 : 128 * (f1 + 1)].reshape(2 * TILE, 128)
                        for f1 in range(4)
                    ],
                    axis=0,
                )
                for s0 in range(4)
            ],
            axis=1,
        )
        done = matmul(lhs, swap_inner[...]).astype(BF16).reshape(4, 2, TILE, 512)
        for f1 in range(4):
            for f0 in range(4):
                for s in range(2):
                    whole[t, field, f1 * 4 + f0, :, 128 * s : 128 * (s + 1)] = done[
                        f1, s, :, 128 * f0 : 128 * (f0 + 1)
                    ]
        to_up(t).start()
        to_down(t).start()
        to_mate(t, 0).start()

    def relay(t):
        to_up(t, down).wait_recv()
        fwd_up(t).start()
        to_mate(t, 1).start()
        to_down(t, up).wait_recv()
        fwd_down(t).start()
        to_mate(t, 2).start()

    def finish(t):
        fwd_up(t, across).wait_recv()
        to_mate(t, 3).start()
        fwd_down(t, across).wait_recv()
        to_mate(t, 4).start()

    def synthesize(t):
        for k in range(5):
            to_mate(t, k, 1).wait_recv()
        lhs = jnp.concatenate(
            [whole[t, s].reshape(TILE * TILE, DEPTH) for s in range(FIELDS)], axis=1
        )
        values = matmul(lhs, basis[...]).astype(BF16).reshape(TILE, TILE, LONS)
        levels = pl.ds(pl.multiple_of(lax.rem(t, GROUPS) * TILE, TILE), TILE)
        lats = pl.ds(pl.multiple_of(t // GROUPS * TILE, TILE), TILE)
        out_ref[levels, lats, :] = values

    size = 128

    def basis_block(i, carry):
        at = pl.ds(pl.multiple_of(i * size, size), size)
        r = i * size + iota((size, 1), 0)
        inside = r % DEPTH
        source = inside // 128 * 16 + inside % 16
        slot = (source * FIELDS + r // DEPTH) * 2 + inside // 64 % 2
        pairs = jnp.broadcast_to(pairs_ref[...].reshape(1, PAIRS), (size, PAIRS))
        pair = jnp.sum(
            jnp.where(iota((size, PAIRS), 1) == slot, pairs, 0).astype(F32), axis=1, keepdims=True
        )
        number = jnp.where(r // 32 % 2 == 0, pair, M - 1.0 - pair)
        part = (r // 16 % 2).astype(F32)
        weight = jnp.where(number == 0.0, 1.0 / math.sqrt(2.0 * M), 2.0 / math.sqrt(2.0 * M))
        longitude = (field * LONS + iota((size, LONS), 1)).astype(F32)
        phase = number * longitude + part * (NLON // 4)
        phase = phase - NLON * jnp.floor(phase * (1.0 / NLON) + 0.5)
        turns = 0.25 - jnp.abs(phase) * (1.0 / NLON)
        square = turns * turns
        value = SINE[-1]
        for c in SINE[-2::-1]:
            value = value * square + c
        value = value * turns
        basis[at, :] = (weight * value).astype(BF16)
        return carry

    def own(p):
        landed[p, wave] = send[wave * PIECES + p]

    def scatter_group(g):
        turn(g)
        if g == 0:
            pl.semaphore_wait(barrier, WAVES + 2)
        scatter(0, g * 128, 128, g)
        lanes = slice(g * 128, (g + 1) * 128)
        landed[0, wave, :, lanes] = send[wave * PIECES, :, lanes]

    scatter_group(0)
    scatter_group(1)

    a, b = iota((512, 512), 0), iota((512, 512), 1)
    keep = a // 16 % 8 * 16
    swap_outer[...] = one_hot(b == a // 4 % 4 * 128 + keep + a // 128 * 4 + a % 4)
    swap_inner[...] = one_hot(b == a % 4 * 128 + keep + a // 4 % 4 * 4 + a // 128)

    scatter_group(2)
    scatter(1, 0, LANES, GROUPS)
    gather(0)
    scatter(2, 0, LANES, GROUPS + 1)
    gather(1)
    relay(0)
    gather(2)
    for p in range(1, PIECES):
        own(p)

    def step(t, carry):
        p, g = t // GROUPS, lax.rem(t, GROUPS)

        @pl.when(t < STEPS + LAG_RELAY)
        def _():
            relay(t - LAG_RELAY)

        @pl.when(jnp.logical_and(g == 0, p < PIECES - 2))
        def _():
            scatter(p + 2, 0, LANES, GROUPS + 1 + p)

        @pl.when(t < STEPS)
        def _():
            gather(t)

        @pl.when(t < STEPS + LAG_FINISH)
        def _():
            finish(t - LAG_FINISH)

        @pl.when(t < BASIS_FROM + BASIS_STEPS)
        def _():
            blocks = FIELDS * DEPTH // size // BASIS_STEPS
            first = (t - BASIS_FROM) * blocks
            lax.fori_loop(first, first + blocks, basis_block, 0)

        @pl.when(jnp.logical_and(t >= BASIS_FROM + BASIS_STEPS, t < CAUGHT_UP))
        def _():
            synthesize(2 * (t - BASIS_FROM - BASIS_STEPS))
            synthesize(2 * (t - BASIS_FROM - BASIS_STEPS) + 1)

        @pl.when(t >= CAUGHT_UP)
        def _():
            synthesize(t - LAG_GRID)

        return carry

    lax.fori_loop(GROUPS, STEPS + LAG_GRID, step, 0)

    for g in range(GROUPS):
        wait_all(0, g * 128, 128, a2a_send.at[g])
    for p in range(1, PIECES):
        wait_all(p, 0, LANES, a2a_send.at[GROUPS - 1 + p])

    def drain(t, carry):
        to_up(t).wait_send()
        to_down(t).wait_send()
        fwd_up(t).wait_send()
        fwd_down(t).wait_send()
        for k in range(5):
            to_mate(t, k).wait_send()
        return carry

    lax.fori_loop(0, STEPS, drain, 0)


def hemisphere_terms(spectral, pair_ids):
    row = jnp.arange(M + 1, dtype=jnp.int32)[None, :]
    boundary = (M - pair_ids)[:, None]
    in_first = row < boundary
    odd = jnp.where(in_first, row, row - boundary) % 2 == 1
    owner = jnp.stack([in_first, jnp.logical_not(in_first)], axis=1)[:, None, :, None, None, :]
    flip = jnp.stack([jnp.zeros_like(odd), odd], axis=1)[:, :, None, None, None, :]
    terms = jnp.where(owner, spectral[:, None], jnp.zeros((), BF16))
    return jnp.where(flip, -terms, terms)


def shards(spectral, legendre, slot_pairs):
    per_device = spectral.shape[0]
    start_slot = lax.axis_index(("wave", "field")) * per_device
    own_pairs = lax.dynamic_slice_in_dim(slot_pairs, start_slot, per_device)
    terms = hemisphere_terms(spectral, own_pairs).reshape(per_device, 2 * HALF, M + 1)
    sums = jnp.einsum("kqr,krj->kqj", terms, legendre, preferred_element_type=F32).astype(BF16)
    dma = pltpu.SemaphoreType.DMA
    vmem = pltpu.VMEM
    return pl.pallas_call(
        kernel,
        out_shape=jax.ShapeDtypeStruct((FLEV, BAND, LONS), BF16),
        in_specs=[pl.BlockSpec(memory_space=pltpu.VMEM)] * 2,
        out_specs=pl.BlockSpec(memory_space=pltpu.VMEM),
        scratch_shapes=[
            vmem((WAVES * PIECES, TILE, LANES), BF16),
            vmem((PIECES, WAVES, TILE, LANES), BF16),
            vmem((STEPS, FIELDS, TILE, TILE, DEPTH), BF16),
            vmem((FIELDS * DEPTH, LONS), BF16),
            vmem((512, 512), BF16),
            vmem((512, 512), BF16),
            dma((GROUPS + PIECES - 1,)), dma((GROUPS + PIECES - 1,)),
            dma((STEPS, 2)), dma((STEPS, 2)),
            dma((STEPS, 2)), dma((STEPS, 2)),
            dma((STEPS, 5)), dma((STEPS, 5)),
        ],
        compiler_params=pltpu.CompilerParams(
            collective_id=0, has_side_effects=True, vmem_limit_bytes=40 << 20
        ),
        name="spectral_to_grid",
    )(slot_pairs, sums)


def solution(mesh):
    in_specs = (P(("wave", "field"), None, None, None, None), P(("wave", "field"), None, None), P())
    out_specs = P(None, "wave", "field")
    return jax.shard_map(shards, mesh=mesh, in_specs=in_specs, out_specs=out_specs, check_vma=False)
```

```python
import math

import jax
import jax.numpy as jnp
from jax import lax
from jax.experimental import pallas as pl
from jax.experimental.pallas import tpu as pltpu
from jax.sharding import PartitionSpec as P

M = 1024
PAIRS = 512
NLON = 5120
NORTH = 1280
FLEV = 48
XS, ZS, YS = 4, 8, 4
WAVES = XS * ZS
FIELDS = 2 * YS
BAND = 80
LONS = 640
TILE = 16
PIECES = BAND // TILE
GROUPS = FLEV // TILE
STEPS = PIECES * GROUPS
ROWS = 128
CHUNKS = M // ROWS
HALF = 4 * FLEV
LANES = 8 * FLEV
DEPTH = 8 * WAVES
LAG_RELAY, LAG_FINISH, LAG_GRID = 2, 3, 4
BASIS_FROM, BASIS_STEPS = 3, 4
EARLY_SEND, EARLY_TURN, EARLY_GRID = 7, 12, 14
CAUGHT_UP = 2 * (BASIS_FROM + BASIS_STEPS) - LAG_GRID
MESH = pl.DeviceIdType.MESH
F32 = jnp.float32
BF16 = jnp.bfloat16
SINE = [(-1.0) ** k * (2.0 * math.pi) ** (2 * k + 1) / math.factorial(2 * k + 1) for k in range(8)]


def iota(shape, dim):
    return lax.broadcasted_iota(jnp.int32, shape, dim)


def one_hot(condition):
    return jnp.where(condition, 1.0, 0.0).astype(BF16)


def matmul(a, b):
    return jnp.dot(a, b, preferred_element_type=F32)


def kernel(
    pairs_hbm, spectral_hbm, legendre_hbm, out_ref,
    pairs_smem, pairs_ref, spectral, mixed_rows, legendre, terms, sums,
    send, early, early_in, landed, whole, basis, swap_outer, swap_inner,
    load_sem, chunk_sem, a2a_send, a2a_recv, early_send, early_recv, y_send, y_recv, fwd_send, fwd_recv, core_send, core_recv,
):
    load_pairs = pltpu.make_async_copy(pairs_hbm, pairs_smem, load_sem.at[0])
    load_spectral = pltpu.make_async_copy(spectral_hbm, spectral, load_sem.at[1])
    load_row = pltpu.make_async_copy(pairs_hbm, pairs_ref, load_sem.at[2])

    def chunk(b, size=ROWS):
        at = pl.ds(b * ROWS, size)
        return pltpu.make_async_copy(legendre_hbm.at[at], mixed_rows.at[at], chunk_sem.at[b])

    load_pairs.start()
    load_spectral.start()
    for b in range(CHUNKS):
        chunk(b).start()
    chunk(CHUNKS, 1).start()
    load_row.start()

    wave = lax.axis_index("wave")
    field = lax.axis_index("field")
    x, z = wave // ZS, wave % ZS
    y, core = field // 2, field % 2
    up = lax.rem(y + 1, YS) * 2 + core
    down = lax.rem(y + YS - 1, YS) * 2 + core
    across = lax.rem(y + 2, YS) * 2 + core
    other = 1 - core
    mate = y * 2 + other

    def peer_of(i):
        return lax.rem(x + i // ZS, XS) * ZS + lax.rem(z + i % ZS, ZS)

    barrier = pltpu.get_barrier_semaphore()
    for there in (up, down, mate):
        pl.semaphore_signal(barrier, inc=1, device_id=(wave, there), device_id_type=MESH)

    def greet(i, carry):
        pl.semaphore_signal(barrier, inc=1, device_id=(peer_of(i), field), device_id_type=MESH)
        return carry

    lax.fori_loop(1, WAVES, greet, 0)

    row = iota((HALF, M + 1), 1)
    first_member = iota((HALF, M + 1), 0) < 2 * FLEV
    load_pairs.wait()
    load_spectral.wait()
    for k in range(2):
        boundary = M - pairs_smem[(wave * FIELDS + field) * 2 + k]
        in_first = row < boundary
        distance = jnp.where(in_first, row, row - boundary)
        own = jnp.where(in_first == first_member, spectral[k].astype(F32), 0.0)
        terms[k, :HALF] = own.astype(BF16)
        terms[k, HALF:] = jnp.where(distance % 2 == 0, own, -own).astype(BF16)

    def separate(b, carry):
        chunk(b).wait()
        at = pl.ds(pl.multiple_of(b * ROWS, ROWS), ROWS)
        a, c = iota((2 * ROWS, 2 * ROWS), 0), iota((2 * ROWS, 2 * ROWS), 1)
        split = one_hot(c == a % ROWS * 2 + a // ROWS)
        both = matmul(split, mixed_rows[at].reshape(2 * ROWS, NORTH)).astype(BF16)
        legendre[0, at] = both[:ROWS]
        legendre[1, at] = both[ROWS:]
        return carry

    mixed_rows[M + 1 :] = jnp.zeros((TILE - 1, 2, NORTH), BF16)
    lax.fori_loop(0, CHUNKS, separate, 0)
    chunk(CHUNKS, 1).wait()
    a, c = iota((2 * TILE, 2 * TILE), 0), iota((2 * TILE, 2 * TILE), 1)
    split = one_hot(c == a % TILE * 2 + a // TILE)
    both = matmul(split, mixed_rows[M:].reshape(2 * TILE, NORTH)).astype(BF16)
    for k in range(2):
        legendre[k, M:] = both[k * TILE : (k + 1) * TILE]
    for k in range(2):
        sums[k] = matmul(terms[k], legendre[k, : M + 1]).astype(BF16)

    def turn(g):
        a, b = iota((256, 256), 0), iota((256, 256), 1)
        for south in range(2):
            pick = one_hot(a + b == 255 if south else a == b)
            for u in range(NORTH // 256):
                start = NORTH - 256 * (u + 1) if south else 256 * u
                rows = [
                    sums[k, lo : lo + TILE, start : start + 256]
                    for k in range(2)
                    for lo in range(south * HALF + g * TILE, (south + 1) * HALF, FLEV)
                ]
                turned = lax.dot_general(
                    pick,
                    jnp.concatenate(rows, axis=0),
                    (((1,), (1,)), ((), ())),
                    preferred_element_type=F32,
                )
                at = south * NORTH // TILE + u * 16
                tiles = turned.astype(BF16).reshape(16, TILE, 128)
                for i in range(16):
                    send[(at + i) // PIECES, (at + i) % PIECES, :, g * 128 : (g + 1) * 128] = tiles[i]

    def scatter(p, lane, lanes, sem):
        def one(i, carry):
            peer = peer_of(i)
            pltpu.make_async_remote_copy(
                src_ref=send.at[peer, p, :, pl.ds(lane, lanes)],
                dst_ref=landed.at[p, wave, :, pl.ds(lane, lanes)],
                send_sem=a2a_send.at[sem],
                recv_sem=a2a_recv.at[sem],
                device_id=(peer, field),
                device_id_type=MESH,
            ).start()
            return carry

        lax.fori_loop(1, WAVES, one, 0)

    def wait_all(p, lane, lanes, sem):
        block = landed.at[p, pl.ds(0, WAVES - 1), :, pl.ds(lane, lanes)]
        pltpu.make_async_copy(block, block, sem).wait()

    def remote(t, source, part, send_sem, recv_sem, slot, there):
        lo, size = ((0, TILE), (0, TILE // 2), (TILE // 2, TILE // 2))[part]
        block = whole.at[t, source, pl.ds(lo, size)]
        return pltpu.make_async_remote_copy(
            src_ref=block, dst_ref=block,
            send_sem=send_sem.at[t, slot], recv_sem=recv_sem.at[t, slot],
            device_id=(wave, there), device_id_type=MESH,
        )

    def to_up(t, part, source=field):
        return remote(t, source, part, y_send, y_recv, part - 1, up)

    def to_down(t, part, source=field):
        return remote(t, source, part, y_send, y_recv, part + 1, down)

    def fwd_up(t, source=down):
        return remote(t, source, 1, fwd_send, fwd_recv, 0, up)

    def fwd_down(t, source=up):
        return remote(t, source, 2, fwd_send, fwd_recv, 1, down)

    def to_mate(t, k, flip=0):
        source, part = ((field, 0), (down, 0), (up, 0), (across, 1), (across, 2))[k]
        if flip:
            source = source // 2 * 2 + other
        return remote(t, source, part, core_send, core_recv, k, mate)

    def shuffle(t, source, got):
        got = got.reshape(2, 4, 4, TILE, 128)
        lhs = jnp.concatenate([got[:, s1].reshape(128, 128) for s1 in range(4)], axis=1)
        mixed = matmul(lhs, swap_outer[...]).astype(BF16).reshape(2, 4, TILE, 512)
        lhs = jnp.concatenate(
            [
                jnp.concatenate(
                    [
                        mixed[:, s0, :, 128 * f1 : 128 * (f1 + 1)].reshape(2 * TILE, 128)
                        for f1 in range(4)
                    ],
                    axis=0,
                )
                for s0 in range(4)
            ],
            axis=1,
        )
        done = matmul(lhs, swap_inner[...]).astype(BF16).reshape(4, 2, TILE, 512)
        for f1 in range(4):
            for f0 in range(4):
                for s in range(2):
                    whole[t, source, f1 * 4 + f0, :, 128 * s : 128 * (s + 1)] = done[
                        f1, s, :, 128 * f0 : 128 * (f0 + 1)
                    ]

    def gather(t):
        p, g = t // GROUPS, lax.rem(t, GROUPS)
        lane = pl.multiple_of(g * 128, 128)

        @pl.when(p < 2)
        def _():
            wait_all(p, lane, 128, a2a_recv.at[t])

        @pl.when(jnp.logical_and(p >= 2, g == 0))
        def _():
            wait_all(p, 0, LANES, a2a_recv.at[2 * GROUPS - 2 + p])

        shuffle(t, field, landed[p, :, :, pl.ds(lane, 128)])
        to_up(t, 1).start()
        to_down(t, 2).start()
        to_up(t, 2).start()
        to_down(t, 1).start()
        to_mate(t, 0).start()

    def relay(t):
        to_up(t, 1, down).wait_recv()
        fwd_up(t).start()
        to_down(t, 2, up).wait_recv()
        fwd_down(t).start()
        to_up(t, 2, down).wait_recv()
        to_mate(t, 1).start()
        to_down(t, 1, up).wait_recv()
        to_mate(t, 2).start()

    def along(source, lo, size, sends, recvs, slot, there):
        block = early.at[source, pl.ds(lo, size)]
        return pltpu.make_async_remote_copy(
            src_ref=block, dst_ref=block, send_sem=sends.at[0, slot], recv_sem=recvs.at[0, slot],
            device_id=(wave, there), device_id_type=MESH,
        )

    def early_up(source=y):
        return along(source, 0, WAVES, y_send, y_recv, 0, up)

    def early_down(source=y):
        return along(source, 0, WAVES, y_send, y_recv, 1, down)

    def early_fwd_up(source=down // 2):
        return along(source, 0, WAVES // 2, fwd_send, fwd_recv, 0, up)

    def early_fwd_down(source=up // 2):
        return along(source, WAVES // 2, WAVES // 2, fwd_send, fwd_recv, 1, down)

    def early_relay():
        early_up(down // 2).wait_recv()
        early_fwd_up().start()
        early_down(up // 2).wait_recv()
        early_fwd_down().start()

    def early_scatter():
        early_fwd_up(across // 2).wait_recv()
        early_fwd_down(across // 2).wait_recv()
        early_in[wave] = early[:, wave]

        def one(i, carry):
            peer = peer_of(i)
            pltpu.make_async_remote_copy(
                src_ref=early.at[:, peer],
                dst_ref=early_in.at[wave],
                send_sem=early_send,
                recv_sem=early_recv,
                device_id=(peer, field),
                device_id_type=MESH,
            ).start()
            return carry

        lax.fori_loop(1, WAVES, one, 0)

    def early_wait(sem):
        block = early_in.at[pl.ds(0, WAVES - 1)]
        pltpu.make_async_copy(block, block, sem).wait()

    def early_mate(source, side):
        return remote(0, source * 2 + side, 0, core_send, core_recv, source, mate)

    def early_turn(source):
        shuffle(0, source * 2 + core, early_in[:, source])
        early_mate(source, core).start()

    def finish(t):
        fwd_up(t, across).wait_recv()
        to_mate(t, 3).start()
        fwd_down(t, across).wait_recv()
        to_mate(t, 4).start()

    def synthesize(t):
        for k in range(5):
            to_mate(t, k, 1).wait_recv()
        product(t)

    def product(t):
        lhs = jnp.concatenate(
            [whole[t, s].reshape(TILE * TILE, DEPTH) for s in range(FIELDS)], axis=1
        )
        values = matmul(lhs, basis[...]).astype(BF16).reshape(TILE, TILE, LONS)
        levels = pl.ds(pl.multiple_of(lax.rem(t, GROUPS) * TILE, TILE), TILE)
        lats = pl.ds(pl.multiple_of(t // GROUPS * TILE, TILE), TILE)
        out_ref[levels, lats, :] = values

    size = 128

    def basis_block(i, carry):
        at = pl.ds(pl.multiple_of(i * size, size), size)
        r = i * size + iota((size, 1), 0)
        inside = r % DEPTH
        source = inside // 128 * 16 + inside % 16
        slot = (source * FIELDS + r // DEPTH) * 2 + inside // 64 % 2
        pairs = jnp.broadcast_to(pairs_ref[...].reshape(1, PAIRS), (size, PAIRS))
        pair = jnp.sum(
            jnp.where(iota((size, PAIRS), 1) == slot, pairs, 0).astype(F32), axis=1, keepdims=True
        )
        number = jnp.where(r // 32 % 2 == 0, pair, M - 1.0 - pair)
        part = (r // 16 % 2).astype(F32)
        weight = jnp.where(number == 0.0, 1.0 / math.sqrt(2.0 * M), 2.0 / math.sqrt(2.0 * M))
        longitude = (field * LONS + iota((size, LONS), 1)).astype(F32)
        phase = number * longitude + part * (NLON // 4)
        phase = phase - NLON * jnp.floor(phase * (1.0 / NLON) + 0.5)
        turns = 0.25 - jnp.abs(phase) * (1.0 / NLON)
        square = turns * turns
        value = SINE[-1]
        for c in SINE[-2::-1]:
            value = value * square + c
        value = value * turns
        basis[at, :] = (weight * value).astype(BF16)
        return carry

    load_row.wait()
    turn(0)
    early[y] = send[:, 0, :, :128]
    pl.semaphore_wait(barrier, WAVES + 2)
    early_up().start()
    early_down().start()
    for g in range(1, GROUPS):
        turn(g)
        scatter(0, g * 128, 128, g)
    a, b = iota((512, 512), 0), iota((512, 512), 1)
    keep = a // 16 % 8 * 16
    swap_outer[...] = one_hot(b == a // 4 % 4 * 128 + keep + a // 128 * 4 + a % 4)
    swap_inner[...] = one_hot(b == a % 4 * 128 + keep + a // 4 % 4 * 4 + a // 128)

    early_relay()
    scatter(1, 0, 128, GROUPS)
    for p in range(PIECES):
        landed[p, wave] = send[wave, p]
    gather(1)
    scatter(1, 128, 128, GROUPS + 1)
    scatter(1, 256, 128, GROUPS + 2)
    gather(2)
    scatter(2, 0, LANES, 2 * GROUPS)

    def step(t, carry):
        p, g = t // GROUPS, lax.rem(t, GROUPS)

        @pl.when(t < STEPS + LAG_RELAY)
        def _():
            relay(t - LAG_RELAY)

        @pl.when(jnp.logical_and(g == 0, p < PIECES - 2))
        def _():
            scatter(p + 2, 0, LANES, 2 * GROUPS + p)

        @pl.when(t < STEPS)
        def _():
            gather(t)

        @pl.when(jnp.logical_and(t > LAG_FINISH, t < STEPS + LAG_FINISH))
        def _():
            finish(t - LAG_FINISH)

        @pl.when(t < BASIS_FROM + BASIS_STEPS)
        def _():
            blocks = FIELDS * DEPTH // size // BASIS_STEPS
            first = (t - BASIS_FROM) * blocks
            lax.fori_loop(first, first + blocks, basis_block, 0)

        @pl.when(t == EARLY_SEND)
        def _():
            early_scatter()

        @pl.when(t == EARLY_TURN)
        def _():
            early_wait(early_recv)

        @pl.when(jnp.logical_and(t >= EARLY_TURN, t < EARLY_TURN + YS // 2))
        def _():
            early_turn(2 * (t - EARLY_TURN))
            early_turn(2 * (t - EARLY_TURN) + 1)

        @pl.when(t == EARLY_GRID)
        def _():
            for source in range(YS):
                early_mate(source, other).wait_recv()
            product(0)

        @pl.when(jnp.logical_and(t > BASIS_FROM + BASIS_STEPS, t < CAUGHT_UP))
        def _():
            synthesize(2 * (t - BASIS_FROM - BASIS_STEPS))

        @pl.when(jnp.logical_and(t >= BASIS_FROM + BASIS_STEPS, t < CAUGHT_UP))
        def _():
            synthesize(2 * (t - BASIS_FROM - BASIS_STEPS) + 1)

        @pl.when(t >= CAUGHT_UP)
        def _():
            synthesize(t - LAG_GRID)

        return carry

    lax.fori_loop(GROUPS, STEPS + LAG_GRID, step, 0)

    for t in range(1, 2 * GROUPS):
        wait_all(t // GROUPS, t % GROUPS * 128, 128, a2a_send.at[t])
    for p in range(2, PIECES):
        wait_all(p, 0, LANES, a2a_send.at[2 * GROUPS - 2 + p])
    early_wait(early_send)
    early_up().wait_send()
    early_down().wait_send()
    early_fwd_up().wait_send()
    early_fwd_down().wait_send()
    for source in range(YS):
        early_mate(source, core).wait_send()

    def drain(t, carry):
        for part in (1, 2):
            to_up(t, part).wait_send()
            to_down(t, part).wait_send()
        fwd_up(t).wait_send()
        fwd_down(t).wait_send()
        for k in range(5):
            to_mate(t, k).wait_send()
        return carry

    lax.fori_loop(1, STEPS, drain, 0)


def shards(spectral, legendre, slot_pairs):
    per_device = spectral.shape[0]
    dma = pltpu.SemaphoreType.DMA
    vmem = pltpu.VMEM
    return pl.pallas_call(
        kernel,
        out_shape=jax.ShapeDtypeStruct((FLEV, BAND, LONS), BF16),
        in_specs=[pl.BlockSpec(memory_space=pltpu.HBM)] * 3,
        out_specs=pl.BlockSpec(memory_space=pltpu.VMEM),
        scratch_shapes=[
            pltpu.SMEM((PAIRS,), jnp.int32),
            vmem((PAIRS,), jnp.int32),
            vmem((per_device, HALF, M + 1), BF16),
            vmem((M + TILE, per_device, NORTH), BF16),
            vmem((per_device, M + TILE, NORTH), BF16),
            vmem((per_device, 2 * HALF, M + 1), BF16),
            vmem((per_device, 2 * HALF, NORTH), BF16),
            vmem((WAVES, PIECES, TILE, LANES), BF16),
            vmem((YS, WAVES, TILE, 128), BF16),
            vmem((WAVES, YS, TILE, 128), BF16),
            vmem((PIECES, WAVES, TILE, LANES), BF16),
            vmem((STEPS, FIELDS, TILE, TILE, DEPTH), BF16),
            vmem((FIELDS * DEPTH, LONS), BF16),
            vmem((512, 512), BF16),
            vmem((512, 512), BF16),
            dma((3,)), dma((CHUNKS + 1,)),
            dma((2 * GROUPS + PIECES - 2,)), dma((2 * GROUPS + PIECES - 2,)),
            dma, dma,
            dma((STEPS, 4)), dma((STEPS, 4)),
            dma((STEPS, 2)), dma((STEPS, 2)),
            dma((STEPS, 5)), dma((STEPS, 5)),
        ],
        compiler_params=pltpu.CompilerParams(
            collective_id=0, has_side_effects=True, vmem_limit_bytes=46 << 20
        ),
        name="spectral_to_grid",
    )(slot_pairs, spectral.reshape(per_device, HALF, M + 1), legendre.transpose(1, 0, 2))


def solution(mesh):
    in_specs = (P(("wave", "field"), None, None, None, None), P(("wave", "field"), None, None), P())
    out_specs = P(None, "wave", "field")
    return jax.shard_map(shards, mesh=mesh, in_specs=in_specs, out_specs=out_specs, check_vma=False)
```

```python
import math

import jax
import jax.numpy as jnp
from jax import lax
from jax.experimental import pallas as pl
from jax.experimental.pallas import tpu as pltpu
from jax.sharding import PartitionSpec as P

M = 1024
PAIRS = 512
NLON = 5120
NORTH = 1280
FLEV = 48
XS, ZS, YS = 4, 8, 4
WAVES = XS * ZS
FIELDS = 2 * YS
BAND = 80
LONS = 640
TILE = 16
PIECES = BAND // TILE
GROUPS = FLEV // TILE
STEPS = PIECES * GROUPS
ROWS = 128
CHUNKS = M // ROWS
HALF = 4 * FLEV
LANES = 8 * FLEV
DEPTH = 8 * WAVES
LAG_RELAY, LAG_GRID = 2, 4
BASIS_FROM, BASIS_STEPS = 3, 4
EARLY_SEND, EARLY_TURN, EARLY_GRID = 7, 12, 14
CAUGHT_UP = 2 * (BASIS_FROM + BASIS_STEPS) - LAG_GRID
MESH = pl.DeviceIdType.MESH
F32 = jnp.float32
BF16 = jnp.bfloat16
SINE = [(-1.0) ** k * (2.0 * math.pi) ** (2 * k + 1) / math.factorial(2 * k + 1) for k in range(8)]


def iota(shape, dim):
    return lax.broadcasted_iota(jnp.int32, shape, dim)


def one_hot(condition):
    return jnp.where(condition, 1.0, 0.0).astype(BF16)


def matmul(a, b):
    return jnp.dot(a, b, preferred_element_type=F32)


def kernel(
    pairs_hbm, spectral_hbm, legendre_hbm, out_ref,
    pairs_smem, pairs_ref, spectral, mixed_rows, legendre, terms, sums,
    send, early, early_in, landed, whole, basis, swap_outer, swap_inner, kept, partial, outgoing, incoming,
    load_sem, chunk_sem, a2a_send, a2a_recv, early_send, early_recv, y_send, y_recv, fwd_send, fwd_recv, core_send, core_recv,
):
    load_pairs = pltpu.make_async_copy(pairs_hbm, pairs_smem, load_sem.at[0])
    load_spectral = pltpu.make_async_copy(spectral_hbm, spectral, load_sem.at[1])
    load_row = pltpu.make_async_copy(pairs_hbm, pairs_ref, load_sem.at[2])

    def chunk(b, size=ROWS):
        at = pl.ds(b * ROWS, size)
        return pltpu.make_async_copy(legendre_hbm.at[at], mixed_rows.at[at], chunk_sem.at[b])

    load_pairs.start()
    load_spectral.start()
    for b in range(CHUNKS):
        chunk(b).start()
    chunk(CHUNKS, 1).start()
    load_row.start()

    wave = lax.axis_index("wave")
    field = lax.axis_index("field")
    x, z = wave // ZS, wave % ZS
    y, core = field // 2, field % 2
    above, below, across = lax.rem(y + 1, YS), lax.rem(y + YS - 1, YS), lax.rem(y + 2, YS)
    up, down, mate = above * 2 + core, below * 2 + core, y * 2 + 1 - core

    def peer_of(i):
        return lax.rem(x + i // ZS, XS) * ZS + lax.rem(z + i % ZS, ZS)

    barrier = pltpu.get_barrier_semaphore()
    for there in (up, down, mate):
        pl.semaphore_signal(barrier, inc=1, device_id=(wave, there), device_id_type=MESH)

    def greet(i, carry):
        pl.semaphore_signal(barrier, inc=1, device_id=(peer_of(i), field), device_id_type=MESH)
        return carry

    lax.fori_loop(1, WAVES, greet, 0)

    row = iota((HALF, M + 1), 1)
    first_member = iota((HALF, M + 1), 0) < 2 * FLEV
    load_pairs.wait()
    load_spectral.wait()
    for k in range(2):
        boundary = M - pairs_smem[(wave * FIELDS + field) * 2 + k]
        in_first = row < boundary
        distance = jnp.where(in_first, row, row - boundary)
        own = jnp.where(in_first == first_member, spectral[k].astype(F32), 0.0)
        mirrored = jnp.where(distance % 2 == 0, own, -own).astype(BF16)
        own = own.astype(BF16)
        for g in range(GROUPS):
            for part in range(4):
                rows = slice(part * FLEV + g * TILE, part * FLEV + (g + 1) * TILE)
                at = g * 128 + part * TILE
                terms[k, at : at + TILE] = own[rows]
                terms[k, at + 64 : at + 64 + TILE] = mirrored[rows]

    def separate(b, carry):
        chunk(b).wait()
        at = pl.ds(pl.multiple_of(b * ROWS, ROWS), ROWS)
        a, c = iota((2 * ROWS, 2 * ROWS), 0), iota((2 * ROWS, 2 * ROWS), 1)
        split = one_hot(c == a % ROWS * 2 + a // ROWS)
        both = matmul(split, mixed_rows[at].reshape(2 * ROWS, NORTH)).astype(BF16)
        legendre[0, at] = both[:ROWS]
        legendre[1, at] = both[ROWS:]
        return carry

    mixed_rows[M + 1 :] = jnp.zeros((TILE - 1, 2, NORTH), BF16)
    lax.fori_loop(0, CHUNKS, separate, 0)
    chunk(CHUNKS, 1).wait()
    a, c = iota((2 * TILE, 2 * TILE), 0), iota((2 * TILE, 2 * TILE), 1)
    split = one_hot(c == a % TILE * 2 + a // TILE)
    both = matmul(split, mixed_rows[M:].reshape(2 * TILE, NORTH)).astype(BF16)
    for k in range(2):
        legendre[k, M:] = both[k * TILE : (k + 1) * TILE]

    def group_sums(g):
        rows = slice(g * 128, (g + 1) * 128)
        for k in range(2):
            sums[k, rows] = matmul(terms[k, rows], legendre[k, : M + 1]).astype(BF16)

    def turn(g):
        a, b = iota((256, 256), 0), iota((256, 256), 1)
        for south in range(2):
            pick = one_hot(a + b == 255 if south else a == b)
            for u in range(NORTH // 256):
                start = NORTH - 256 * (u + 1) if south else 256 * u
                rows = [
                    sums[k, lo : lo + TILE, start : start + 256]
                    for k in range(2)
                    for lo in range(g * 128 + south * 64, g * 128 + south * 64 + 64, TILE)
                ]
                turned = lax.dot_general(
                    pick,
                    jnp.concatenate(rows, axis=0),
                    (((1,), (1,)), ((), ())),
                    preferred_element_type=F32,
                )
                at = south * NORTH // TILE + u * 16
                tiles = turned.astype(BF16).reshape(16, TILE, 128)
                for i in range(16):
                    send[(at + i) // PIECES, (at + i) % PIECES, :, g * 128 : (g + 1) * 128] = tiles[i]

    def scatter(p, lane, lanes, sem):
        def one(i, carry):
            peer = peer_of(i)
            pltpu.make_async_remote_copy(
                src_ref=send.at[peer, p, :, pl.ds(lane, lanes)],
                dst_ref=landed.at[p, wave, :, pl.ds(lane, lanes)],
                send_sem=a2a_send.at[sem],
                recv_sem=a2a_recv.at[sem],
                device_id=(peer, field),
                device_id_type=MESH,
            ).start()
            return carry

        lax.fori_loop(1, WAVES, one, 0)

    def wait_all(p, lane, lanes, sem):
        block = landed.at[p, pl.ds(0, WAVES - 1), :, pl.ds(lane, lanes)]
        pltpu.make_async_copy(block, block, sem).wait()

    def remote(t, source, part, send_sem, recv_sem, slot, there):
        lo, size = ((0, TILE), (0, TILE // 2), (TILE // 2, TILE // 2))[part]
        block = whole.at[t, source, pl.ds(lo, size)]
        return pltpu.make_async_remote_copy(
            src_ref=block, dst_ref=block,
            send_sem=send_sem.at[t, slot], recv_sem=recv_sem.at[t, slot],
            device_id=(wave, there), device_id_type=MESH,
        )

    def to_up(t, part, source=y):
        return remote(t, source, part, y_send, y_recv, part - 1, up)

    def to_down(t, part, source=y):
        return remote(t, source, part, y_send, y_recv, part + 1, down)

    def fwd_up(t, source=below):
        return remote(t, source, 1, fwd_send, fwd_recv, 0, up)

    def fwd_down(t, source=above):
        return remote(t, source, 2, fwd_send, fwd_recv, 1, down)

    def to_mate(t):
        return pltpu.make_async_remote_copy(
            src_ref=outgoing.at[t], dst_ref=incoming.at[t],
            send_sem=core_send.at[t], recv_sem=core_recv.at[t],
            device_id=(wave, mate), device_id_type=MESH,
        )

    def shuffle(t, source, got):
        got = got.reshape(2, 4, 4, TILE, 128)
        lhs = jnp.concatenate([got[:, s1].reshape(128, 128) for s1 in range(4)], axis=1)
        mixed = matmul(lhs, swap_outer[...]).astype(BF16).reshape(2, 4, TILE, 512)
        lhs = jnp.concatenate(
            [
                jnp.concatenate(
                    [
                        mixed[:, s0, :, 128 * f1 : 128 * (f1 + 1)].reshape(2 * TILE, 128)
                        for f1 in range(4)
                    ],
                    axis=0,
                )
                for s0 in range(4)
            ],
            axis=1,
        )
        done = matmul(lhs, swap_inner[...]).astype(BF16).reshape(4, 2, TILE, 512)
        for f1 in range(4):
            for f0 in range(4):
                for s in range(2):
                    whole[t, source, f1 * 4 + f0, :, 128 * s : 128 * (s + 1)] = done[
                        f1, s, :, 128 * f0 : 128 * (f0 + 1)
                    ]

    def gather(t):
        p, g = t // GROUPS, lax.rem(t, GROUPS)
        lane = pl.multiple_of(g * 128, 128)

        @pl.when(p < 2)
        def _():
            wait_all(p, lane, 128, a2a_recv.at[t])

        @pl.when(jnp.logical_and(p >= 2, g == 0))
        def _():
            wait_all(p, 0, LANES, a2a_recv.at[2 * GROUPS - 2 + p])

        shuffle(t, y, landed[p, :, :, pl.ds(lane, 128)])
        to_up(t, 1).start()
        to_down(t, 2).start()
        to_up(t, 2).start()
        to_down(t, 1).start()

    def relay(t):
        to_up(t, 1, below).wait_recv()
        fwd_up(t).start()
        to_down(t, 2, above).wait_recv()
        fwd_down(t).start()

    def along(source, lo, size, sends, recvs, slot, there):
        block = early.at[source, pl.ds(lo, size)]
        return pltpu.make_async_remote_copy(
            src_ref=block, dst_ref=block, send_sem=sends.at[0, slot], recv_sem=recvs.at[0, slot],
            device_id=(wave, there), device_id_type=MESH,
        )

    def early_up(source=y):
        return along(source, 0, WAVES, y_send, y_recv, 0, up)

    def early_down(source=y):
        return along(source, 0, WAVES, y_send, y_recv, 1, down)

    def early_fwd_up(source=below):
        return along(source, 0, WAVES // 2, fwd_send, fwd_recv, 0, up)

    def early_fwd_down(source=above):
        return along(source, WAVES // 2, WAVES // 2, fwd_send, fwd_recv, 1, down)

    def early_relay():
        early_up(below).wait_recv()
        early_fwd_up().start()
        early_down(above).wait_recv()
        early_fwd_down().start()

    def early_scatter():
        early_fwd_up(across).wait_recv()
        early_fwd_down(across).wait_recv()
        early_in[wave] = early[:, wave]

        def one(i, carry):
            peer = peer_of(i)
            pltpu.make_async_remote_copy(
                src_ref=early.at[:, peer],
                dst_ref=early_in.at[wave],
                send_sem=early_send,
                recv_sem=early_recv,
                device_id=(peer, field),
                device_id_type=MESH,
            ).start()
            return carry

        lax.fori_loop(1, WAVES, one, 0)

    def early_wait(sem):
        block = early_in.at[pl.ds(0, WAVES - 1)]
        pltpu.make_async_copy(block, block, sem).wait()

    def split(t, slot, values):
        outgoing[t] = values[:, LONS:].astype(BF16).reshape(TILE, TILE, LONS)
        to_mate(t).start()
        kept[slot] = values[:, :LONS]

    def columns(t, source):
        return whole[t, source].reshape(TILE * TILE, DEPTH)

    def product(t, slot):
        lhs = jnp.concatenate([columns(t, s) for s in range(YS)], axis=1)
        split(t, slot, matmul(lhs, basis[...]))

    def synthesize(t):
        to_up(t, 2, below).wait_recv()
        to_down(t, 1, above).wait_recv()
        fwd_up(t, across).wait_recv()
        fwd_down(t, across).wait_recv()
        product(t, lax.rem(t, 2))

    def combine(t, slot):
        to_mate(t).wait_recv()
        values = kept[slot] + incoming[t].reshape(TILE * TILE, LONS).astype(F32)
        levels = pl.ds(pl.multiple_of(lax.rem(t, GROUPS) * TILE, TILE), TILE)
        lats = pl.ds(pl.multiple_of(t // GROUPS * TILE, TILE), TILE)
        out_ref[levels, lats, :] = values.astype(BF16).reshape(TILE, TILE, LONS)

    size = 128

    def basis_block(i, carry):
        at = pl.ds(pl.multiple_of(i * size, size), size)
        r = i * size + iota((size, 1), 0)
        inside = r % DEPTH
        source = inside // 128 * 16 + inside % 16
        slot = (source * FIELDS + r // DEPTH * 2 + core) * 2 + inside // 64 % 2
        pairs = jnp.broadcast_to(pairs_ref[...].reshape(1, PAIRS), (size, PAIRS))
        pair = jnp.sum(
            jnp.where(iota((size, PAIRS), 1) == slot, pairs, 0).astype(F32), axis=1, keepdims=True
        )
        number = jnp.where(r // 32 % 2 == 0, pair, M - 1.0 - pair)
        part = (r // 16 % 2).astype(F32)
        weight = jnp.where(number == 0.0, 1.0 / math.sqrt(2.0 * M), 2.0 / math.sqrt(2.0 * M))
        column = iota((size, 2 * LONS), 1)
        longitude = jnp.where(column < LONS, field * LONS + column, (mate - 1) * LONS + column)
        longitude = longitude.astype(F32)
        phase = number * longitude + part * (NLON // 4)
        phase = phase - NLON * jnp.floor(phase * (1.0 / NLON) + 0.5)
        turns = 0.25 - jnp.abs(phase) * (1.0 / NLON)
        square = turns * turns
        value = SINE[-1]
        for c in SINE[-2::-1]:
            value = value * square + c
        value = value * turns
        basis[at, :] = (weight * value).astype(BF16)
        return carry

    load_row.wait()
    group_sums(1)
    turn(1)
    pl.semaphore_wait(barrier, WAVES + 2)
    scatter(0, 128, 128, 1)
    group_sums(0)
    turn(0)
    early[y] = send[:, 0, :, :128]
    early_up().start()
    early_down().start()
    group_sums(2)
    turn(2)
    scatter(0, 256, 128, 2)
    a, b = iota((512, 512), 0), iota((512, 512), 1)
    keep = a // 16 % 8 * 16
    swap_outer[...] = one_hot(b == a // 4 % 4 * 128 + keep + a // 128 * 4 + a % 4)
    swap_inner[...] = one_hot(b == a % 4 * 128 + keep + a // 4 % 4 * 4 + a // 128)

    early_relay()
    scatter(1, 0, 128, GROUPS)
    for p in range(PIECES):
        landed[p, wave] = send[wave, p]
    gather(1)
    scatter(1, 128, 128, GROUPS + 1)
    scatter(1, 256, 128, GROUPS + 2)
    gather(2)
    scatter(2, 0, LANES, 2 * GROUPS)

    def step(t, carry):
        p, g = t // GROUPS, lax.rem(t, GROUPS)

        @pl.when(t < STEPS + LAG_RELAY)
        def _():
            relay(t - LAG_RELAY)

        @pl.when(jnp.logical_and(g == 0, p < PIECES - 2))
        def _():
            scatter(p + 2, 0, LANES, 2 * GROUPS + p)

        @pl.when(t < STEPS)
        def _():
            gather(t)

        @pl.when(t < BASIS_FROM + BASIS_STEPS)
        def _():
            blocks = YS * DEPTH // size // BASIS_STEPS
            first = (t - BASIS_FROM) * blocks
            lax.fori_loop(first, first + blocks, basis_block, 0)

        @pl.when(t == EARLY_SEND)
        def _():
            early_scatter()

        @pl.when(t == EARLY_TURN)
        def _():
            early_wait(early_recv)

        @pl.when(jnp.logical_and(t >= EARLY_TURN, t < EARLY_TURN + YS // 2))
        def _():
            for i in range(2):
                source = 2 * (t - EARLY_TURN) + i
                shuffle(0, source, early_in[:, source])

        @pl.when(t == EARLY_GRID)
        def _():
            product(0, 2)

        @pl.when(jnp.logical_and(t > BASIS_FROM + BASIS_STEPS, t < CAUGHT_UP))
        def _():
            n = 2 * (t - BASIS_FROM - BASIS_STEPS)
            synthesize(n)
            combine(n - 1, 1)

        @pl.when(t >= BASIS_FROM + BASIS_STEPS)
        def _():
            n = jnp.where(t < CAUGHT_UP, 2 * (t - BASIS_FROM - BASIS_STEPS) + 1, t - LAG_GRID)
            synthesize(n)

            @pl.when(n > 1)
            def _():
                combine(n - 1, lax.rem(n - 1, 2))

        return carry

    lax.fori_loop(GROUPS, STEPS + LAG_RELAY, step, 0)

    last = STEPS - 1

    def last_sum(sources):
        rows = [pl.ds(pl.multiple_of(s * DEPTH, DEPTH), DEPTH) for s in sources]
        return matmul(
            jnp.concatenate([columns(last, s) for s in sources], axis=1),
            jnp.concatenate([basis[at, :] for at in rows], axis=0),
        )

    synthesize(last - 1)
    combine(last - 2, last % 2)
    to_up(last, 2, below).wait_recv()
    to_down(last, 1, above).wait_recv()
    partial[...] = last_sum([y, below, above])
    fwd_up(last, across).wait_recv()
    fwd_down(last, across).wait_recv()
    split(last, last % 2, partial[...] + last_sum([across]))
    combine(last - 1, (last - 1) % 2)
    combine(0, 2)
    combine(last, last % 2)

    for t in range(1, 2 * GROUPS):
        wait_all(t // GROUPS, t % GROUPS * 128, 128, a2a_send.at[t])
    for p in range(2, PIECES):
        wait_all(p, 0, LANES, a2a_send.at[2 * GROUPS - 2 + p])
    early_wait(early_send)
    early_up().wait_send()
    early_down().wait_send()
    early_fwd_up().wait_send()
    early_fwd_down().wait_send()
    to_mate(0).wait_send()

    def drain(t, carry):
        for part in (1, 2):
            to_up(t, part).wait_send()
            to_down(t, part).wait_send()
        fwd_up(t).wait_send()
        fwd_down(t).wait_send()
        to_mate(t).wait_send()
        return carry

    lax.fori_loop(1, STEPS, drain, 0)


def shards(spectral, legendre, slot_pairs):
    per_device = spectral.shape[0]
    dma = pltpu.SemaphoreType.DMA
    vmem = pltpu.VMEM
    return pl.pallas_call(
        kernel,
        out_shape=vmem((FLEV, BAND, LONS), BF16),
        in_specs=[pl.BlockSpec(memory_space=pltpu.HBM)] * 3,
        out_specs=pl.BlockSpec(memory_space=pltpu.VMEM),
        scratch_shapes=[
            pltpu.SMEM((PAIRS,), jnp.int32),
            vmem((PAIRS,), jnp.int32),
            vmem((per_device, HALF, M + 1), BF16),
            vmem((M + TILE, per_device, NORTH), BF16),
            vmem((per_device, M + TILE, NORTH), BF16),
            vmem((per_device, 2 * HALF, M + 1), BF16),
            vmem((per_device, 2 * HALF, NORTH), BF16),
            vmem((WAVES, PIECES, TILE, LANES), BF16),
            vmem((YS, WAVES, TILE, 128), BF16),
            vmem((WAVES, YS, TILE, 128), BF16),
            vmem((PIECES, WAVES, TILE, LANES), BF16),
            vmem((STEPS, YS, TILE, TILE, DEPTH), BF16),
            vmem((YS * DEPTH, 2 * LONS), BF16),
            vmem((512, 512), BF16),
            vmem((512, 512), BF16),
            vmem((3, TILE * TILE, LONS), F32),
            vmem((TILE * TILE, 2 * LONS), F32),
            vmem((STEPS, TILE, TILE, LONS), BF16),
            vmem((STEPS, TILE, TILE, LONS), BF16),
            dma((3,)), dma((CHUNKS + 1,)),
            dma((2 * GROUPS + PIECES - 2,)), dma((2 * GROUPS + PIECES - 2,)),
            dma, dma,
            dma((STEPS, 4)), dma((STEPS, 4)),
            dma((STEPS, 2)), dma((STEPS, 2)),
            dma((STEPS,)), dma((STEPS,)),
        ],
        compiler_params=pltpu.CompilerParams(
            collective_id=0, has_side_effects=True, vmem_limit_bytes=50 << 20
        ),
        name="spectral_to_grid",
    )(
        pltpu.with_memory_space_constraint(slot_pairs, pltpu.HBM),
        pltpu.with_memory_space_constraint(spectral.reshape(per_device, HALF, M + 1), pltpu.HBM),
        pltpu.with_memory_space_constraint(legendre.transpose(1, 0, 2), pltpu.HBM),
    )


def solution(mesh):
    in_specs = (P(("wave", "field"), None, None, None, None), P(("wave", "field"), None, None), P())
    out_specs = P(None, "wave", "field")
    return jax.shard_map(shards, mesh=mesh, in_specs=in_specs, out_specs=out_specs, check_vma=False)
```

```python
import math

import jax
import jax.numpy as jnp
from jax import lax
from jax.experimental import pallas as pl
from jax.experimental.pallas import tpu as pltpu
from jax.sharding import PartitionSpec as P

M = 1024
PAIRS = 512
NLON = 5120
NORTH = 1280
FLEV = 48
XS, ZS, YS = 4, 8, 4
WAVES = XS * ZS
FIELDS = 2 * YS
BAND = 80
LONS = 640
TILE = 16
PIECES = BAND // TILE
GROUPS = FLEV // TILE
STEPS = PIECES * GROUPS
ROWS = 128
CHUNKS = M // ROWS
HALF = 4 * FLEV
LANES = 8 * FLEV
DEPTH = 8 * WAVES
LAG_RELAY, LAG_GRID = 2, 4
BASIS_FROM, BASIS_STEPS = 3, 4
EARLY_SEND, EARLY_TURN, EARLY_GRID = 8, 13, 15
CAUGHT_UP = 2 * (BASIS_FROM + BASIS_STEPS) - LAG_GRID
MESH = pl.DeviceIdType.MESH
F32 = jnp.float32
BF16 = jnp.bfloat16
SINE = [(-1.0) ** k * (2.0 * math.pi) ** (2 * k + 1) / math.factorial(2 * k + 1) for k in range(8)]


def iota(shape, dim):
    return lax.broadcasted_iota(jnp.int32, shape, dim)


def one_hot(condition):
    return jnp.where(condition, 1.0, 0.0).astype(BF16)


def matmul(a, b):
    return jnp.dot(a, b, preferred_element_type=F32)


def kernel(
    pairs_hbm, spectral_hbm, legendre_hbm, out_ref,
    pairs_smem, pairs_ref, spectral, mixed_rows, legendre, terms, sums,
    send, early, early_in, landed, whole, basis, swap_outer, swap_inner, kept, partial, outgoing, incoming,
    load_sem, chunk_sem, a2a_send, a2a_recv, early_send, early_recv, y_send, y_recv, fwd_send, fwd_recv, core_send, core_recv,
):
    load_pairs = pltpu.make_async_copy(pairs_hbm, pairs_smem, load_sem.at[0])
    load_spectral = pltpu.make_async_copy(spectral_hbm, spectral, load_sem.at[1])
    load_row = pltpu.make_async_copy(pairs_hbm, pairs_ref, load_sem.at[2])

    def chunk(b, size=ROWS):
        at = pl.ds(b * ROWS, size)
        return pltpu.make_async_copy(legendre_hbm.at[at], mixed_rows.at[at], chunk_sem.at[b])

    load_pairs.start()
    load_spectral.start()
    for b in range(CHUNKS):
        chunk(b).start()
    chunk(CHUNKS, 1).start()
    load_row.start()

    wave = lax.axis_index("wave")
    field = lax.axis_index("field")
    x, z = wave // ZS, wave % ZS
    y, core = field // 2, field % 2
    above, below, across = lax.rem(y + 1, YS), lax.rem(y + YS - 1, YS), lax.rem(y + 2, YS)
    up, down, mate = above * 2 + core, below * 2 + core, y * 2 + 1 - core

    def peer_of(i):
        return lax.rem(x + i // ZS, XS) * ZS + lax.rem(z + i % ZS, ZS)

    barrier = pltpu.get_barrier_semaphore()
    for there in (up, down, mate):
        pl.semaphore_signal(barrier, inc=1, device_id=(wave, there), device_id_type=MESH)

    def greet(i, carry):
        pl.semaphore_signal(barrier, inc=1, device_id=(peer_of(i), field), device_id_type=MESH)
        return carry

    lax.fori_loop(1, WAVES, greet, 0)

    a, c = iota((2 * ROWS, 2 * ROWS), 0), iota((2 * ROWS, 2 * ROWS), 1)
    swap_outer[: 2 * ROWS, : 2 * ROWS] = one_hot(c == a % ROWS * 2 + a // ROWS)
    mixed_rows[M + 1 :] = jnp.zeros((TILE - 1, 2, NORTH), BF16)

    row = iota((TILE, M + 1), 1)
    load_pairs.wait()
    load_spectral.wait()
    for k in range(2):
        boundary = M - pairs_smem[(wave * FIELDS + field) * 2 + k]
        in_first = row < boundary
        odd = jnp.where(in_first, row, row - boundary) % 2 == 1
        owners = [one_hot(in_first), one_hot(jnp.logical_not(in_first))]
        sign = jnp.where(odd, -1.0, 1.0).astype(BF16)
        for part in range(4):
            for g in range(GROUPS):
                at = g * 128 + part * TILE
                lo = part * FLEV + g * TILE
                own = spectral[k, lo : lo + TILE] * owners[part // 2]
                terms[k, at : at + TILE] = own
                terms[k, at + 64 : at + 64 + TILE] = own * sign

    def separate(i, carry):
        for n in range(2):
            b = 2 * i + n
            chunk(b).wait()
            at = pl.ds(pl.multiple_of(b * ROWS, ROWS), ROWS)
            rows = mixed_rows[at].reshape(2 * ROWS, NORTH)
            both = matmul(swap_outer[: 2 * ROWS, : 2 * ROWS], rows).astype(BF16)
            legendre[0, at] = both[:ROWS]
            legendre[1, at] = both[ROWS:]
        return carry

    lax.fori_loop(0, CHUNKS // 2, separate, 0)
    chunk(CHUNKS, 1).wait()
    a, c = iota((2 * TILE, 2 * TILE), 0), iota((2 * TILE, 2 * TILE), 1)
    split = one_hot(c == a % TILE * 2 + a // TILE)
    both = matmul(split, mixed_rows[M:].reshape(2 * TILE, NORTH)).astype(BF16)
    for k in range(2):
        legendre[k, M:] = both[k * TILE : (k + 1) * TILE]

    def group_sums(g):
        rows = slice(g * 128, (g + 1) * 128)
        for k in range(2):
            sums[k, rows] = matmul(terms[k, rows], legendre[k, : M + 1]).astype(BF16)

    def turn(g):
        a, b = iota((256, 256), 0), iota((256, 256), 1)
        for south in range(2):
            pick = one_hot(a + b == 255 if south else a == b)
            for u in range(NORTH // 256):
                start = NORTH - 256 * (u + 1) if south else 256 * u
                rows = [
                    sums[k, lo : lo + TILE, start : start + 256]
                    for k in range(2)
                    for lo in range(g * 128 + south * 64, g * 128 + south * 64 + 64, TILE)
                ]
                turned = lax.dot_general(
                    pick,
                    jnp.concatenate(rows, axis=0),
                    (((1,), (1,)), ((), ())),
                    preferred_element_type=F32,
                )
                at = south * NORTH // TILE + u * 16
                tiles = turned.astype(BF16).reshape(16, TILE, 128)
                for i in range(16):
                    send[(at + i) // PIECES, (at + i) % PIECES, :, g * 128 : (g + 1) * 128] = tiles[i]

    def scatter(p, lane, lanes, sem):
        def one(i, carry):
            peer = peer_of(i)
            pltpu.make_async_remote_copy(
                src_ref=send.at[peer, p, :, pl.ds(lane, lanes)],
                dst_ref=landed.at[p, wave, :, pl.ds(lane, lanes)],
                send_sem=a2a_send.at[sem],
                recv_sem=a2a_recv.at[sem],
                device_id=(peer, field),
                device_id_type=MESH,
            ).start()
            return carry

        lax.fori_loop(1, WAVES, one, 0)

    def wait_all(p, lane, lanes, sem):
        block = landed.at[p, pl.ds(0, WAVES - 1), :, pl.ds(lane, lanes)]
        pltpu.make_async_copy(block, block, sem).wait()

    def remote(t, source, part, send_sem, recv_sem, slot, there):
        lo, size = ((0, TILE), (0, TILE // 2), (TILE // 2, TILE // 2))[part]
        block = whole.at[t, source, pl.ds(lo, size)]
        return pltpu.make_async_remote_copy(
            src_ref=block, dst_ref=block,
            send_sem=send_sem.at[t, slot], recv_sem=recv_sem.at[t, slot],
            device_id=(wave, there), device_id_type=MESH,
        )

    def to_up(t, part, source=y):
        return remote(t, source, part, y_send, y_recv, part - 1, up)

    def to_down(t, part, source=y):
        return remote(t, source, part, y_send, y_recv, part + 1, down)

    def fwd_up(t, source=below):
        return remote(t, source, 1, fwd_send, fwd_recv, 0, up)

    def fwd_down(t, source=above):
        return remote(t, source, 2, fwd_send, fwd_recv, 1, down)

    def to_mate(t):
        return pltpu.make_async_remote_copy(
            src_ref=outgoing.at[t], dst_ref=incoming.at[t],
            send_sem=core_send.at[t], recv_sem=core_recv.at[t],
            device_id=(wave, mate), device_id_type=MESH,
        )

    def half_to_mate(half):
        block = pl.ds(half * TILE // 2, TILE // 2)
        return pltpu.make_async_remote_copy(
            src_ref=outgoing.at[STEPS - 1, block], dst_ref=incoming.at[STEPS - 1, block],
            send_sem=core_send.at[STEPS - 1 + half], recv_sem=core_recv.at[STEPS - 1 + half],
            device_id=(wave, mate), device_id_type=MESH,
        )

    def shuffle(t, source, got):
        got = got.reshape(2, 4, 4, TILE, 128)
        lhs = jnp.concatenate([got[:, s1].reshape(128, 128) for s1 in range(4)], axis=1)
        mixed = matmul(lhs, swap_outer[...]).astype(BF16).reshape(2, 4, TILE, 512)
        lhs = jnp.concatenate(
            [
                jnp.concatenate(
                    [
                        mixed[:, s0, :, 128 * f1 : 128 * (f1 + 1)].reshape(2 * TILE, 128)
                        for f1 in range(4)
                    ],
                    axis=0,
                )
                for s0 in range(4)
            ],
            axis=1,
        )
        done = matmul(lhs, swap_inner[...]).astype(BF16).reshape(4, 2, TILE, 512)
        for f1 in range(4):
            for f0 in range(4):
                for s in range(2):
                    whole[t, source, f1 * 4 + f0, :, 128 * s : 128 * (s + 1)] = done[
                        f1, s, :, 128 * f0 : 128 * (f0 + 1)
                    ]

    def gather(t):
        p, g = t // GROUPS, lax.rem(t, GROUPS)
        lane = pl.multiple_of(g * 128, 128)

        @pl.when(p < 2)
        def _():
            wait_all(p, lane, 128, a2a_recv.at[t])

        @pl.when(jnp.logical_and(p >= 2, g == 0))
        def _():
            wait_all(p, 0, LANES, a2a_recv.at[2 * GROUPS - 2 + p])

        shuffle(t, y, landed[p, :, :, pl.ds(lane, 128)])
        to_up(t, 1).start()
        to_down(t, 2).start()
        to_up(t, 2).start()
        to_down(t, 1).start()

    def relay(t):
        to_up(t, 1, below).wait_recv()
        fwd_up(t).start()
        to_down(t, 2, above).wait_recv()
        fwd_down(t).start()

    def along(source, lo, size, sends, recvs, slot, there):
        block = early.at[source, pl.ds(lo, size)]
        return pltpu.make_async_remote_copy(
            src_ref=block, dst_ref=block, send_sem=sends.at[0, slot], recv_sem=recvs.at[0, slot],
            device_id=(wave, there), device_id_type=MESH,
        )

    def early_up(source=y):
        return along(source, 0, WAVES, y_send, y_recv, 0, up)

    def early_down(source=y):
        return along(source, 0, WAVES, y_send, y_recv, 1, down)

    def early_fwd_up(source=below):
        return along(source, 0, WAVES // 2, fwd_send, fwd_recv, 0, up)

    def early_fwd_down(source=above):
        return along(source, WAVES // 2, WAVES // 2, fwd_send, fwd_recv, 1, down)

    def early_relay():
        early_up(below).wait_recv()
        early_fwd_up().start()
        early_down(above).wait_recv()
        early_fwd_down().start()

    def early_scatter():
        early_fwd_up(across).wait_recv()
        early_fwd_down(across).wait_recv()
        early_in[wave] = early[:, wave]

        def one(i, carry):
            peer = peer_of(i)
            pltpu.make_async_remote_copy(
                src_ref=early.at[:, peer],
                dst_ref=early_in.at[wave],
                send_sem=early_send,
                recv_sem=early_recv,
                device_id=(peer, field),
                device_id_type=MESH,
            ).start()
            return carry

        lax.fori_loop(1, WAVES, one, 0)

    def early_wait(sem):
        block = early_in.at[pl.ds(0, WAVES - 1)]
        pltpu.make_async_copy(block, block, sem).wait()

    def split(t, slot, values):
        outgoing[t] = values[:, LONS:].astype(BF16).reshape(TILE, TILE, LONS)
        to_mate(t).start()
        kept[slot] = values[:, :LONS]

    def columns(t, source):
        return whole[t, source].reshape(TILE * TILE, DEPTH)

    def product(t, slot):
        lhs = jnp.concatenate([columns(t, s) for s in range(YS)], axis=1)
        split(t, slot, matmul(lhs, basis[...]))

    def synthesize(t):
        to_up(t, 2, below).wait_recv()
        to_down(t, 1, above).wait_recv()
        fwd_up(t, across).wait_recv()
        fwd_down(t, across).wait_recv()
        product(t, lax.rem(t, 2))

    def combine(t, slot):
        to_mate(t).wait_recv()
        settle(t, slot)

    def settle(t, slot):
        values = kept[slot] + incoming[t].reshape(TILE * TILE, LONS).astype(F32)
        levels = pl.ds(pl.multiple_of(lax.rem(t, GROUPS) * TILE, TILE), TILE)
        lats = pl.ds(pl.multiple_of(t // GROUPS * TILE, TILE), TILE)
        out_ref[levels, lats, :] = values.astype(BF16).reshape(TILE, TILE, LONS)

    size = 128

    def basis_block(i, carry):
        at = pl.ds(pl.multiple_of(i * size, size), size)
        r = i * size + iota((size, 1), 0)
        inside = r % DEPTH
        source = inside // 128 * 16 + inside % 16
        slot = (source * FIELDS + r // DEPTH * 2 + core) * 2 + inside // 64 % 2
        pairs = jnp.broadcast_to(pairs_ref[...].reshape(1, PAIRS), (size, PAIRS))
        pair = jnp.sum(
            jnp.where(iota((size, PAIRS), 1) == slot, pairs, 0).astype(F32), axis=1, keepdims=True
        )
        number = jnp.where(r // 32 % 2 == 0, pair, M - 1.0 - pair)
        part = (r // 16 % 2).astype(F32)
        weight = jnp.where(number == 0.0, 1.0 / math.sqrt(2.0 * M), 2.0 / math.sqrt(2.0 * M))
        column = iota((size, 2 * LONS), 1)
        longitude = jnp.where(column < LONS, field * LONS + column, (mate - 1) * LONS + column)
        longitude = longitude.astype(F32)
        phase = number * longitude + part * (NLON // 4)
        phase = phase - NLON * jnp.floor(phase * (1.0 / NLON) + 0.5)
        turns = 0.25 - jnp.abs(phase) * (1.0 / NLON)
        square = turns * turns
        value = SINE[-1]
        for c in SINE[-2::-1]:
            value = value * square + c
        value = value * turns
        basis[at, :] = (weight * value).astype(BF16)
        return carry

    load_row.wait()
    group_sums(1)
    turn(1)
    pl.semaphore_wait(barrier, WAVES + 2)
    scatter(0, 128, 128, 1)
    group_sums(0)
    turn(0)
    early[y] = send[:, 0, :, :128]
    early_up().start()
    early_down().start()
    group_sums(2)
    turn(2)
    scatter(0, 256, 128, 2)
    a, b = iota((512, 512), 0), iota((512, 512), 1)
    keep = a // 16 % 8 * 16
    swap_outer[...] = one_hot(b == a // 4 % 4 * 128 + keep + a // 128 * 4 + a % 4)
    swap_inner[...] = one_hot(b == a % 4 * 128 + keep + a // 4 % 4 * 4 + a // 128)

    early_relay()
    scatter(1, 0, 128, GROUPS)
    for p in range(PIECES):
        landed[p, wave] = send[wave, p]
    gather(1)
    scatter(1, 128, 128, GROUPS + 1)
    scatter(1, 256, 128, GROUPS + 2)
    gather(2)
    scatter(2, 0, LANES, 2 * GROUPS)

    def step(t, carry):
        p, g = t // GROUPS, lax.rem(t, GROUPS)

        @pl.when(t < STEPS + LAG_RELAY)
        def _():
            relay(t - LAG_RELAY)

        @pl.when(jnp.logical_and(g == 0, p < PIECES - 2))
        def _():
            scatter(p + 2, 0, LANES, 2 * GROUPS + p)

        @pl.when(t < STEPS)
        def _():
            gather(t)

        @pl.when(t < BASIS_FROM + BASIS_STEPS)
        def _():
            blocks = YS * DEPTH // size // BASIS_STEPS
            first = (t - BASIS_FROM) * blocks
            lax.fori_loop(first, first + blocks, basis_block, 0)

        @pl.when(t == EARLY_SEND)
        def _():
            early_scatter()

        @pl.when(t == EARLY_TURN)
        def _():
            early_wait(early_recv)

        @pl.when(jnp.logical_and(t >= EARLY_TURN, t < EARLY_TURN + YS // 2))
        def _():
            for i in range(2):
                source = 2 * (t - EARLY_TURN) + i
                shuffle(0, source, early_in[:, source])

        @pl.when(t == EARLY_GRID)
        def _():
            product(0, 2)

        @pl.when(jnp.logical_and(t > BASIS_FROM + BASIS_STEPS, t < CAUGHT_UP))
        def _():
            n = 2 * (t - BASIS_FROM - BASIS_STEPS)
            synthesize(n)
            combine(n - 1, 1)

        @pl.when(t >= BASIS_FROM + BASIS_STEPS)
        def _():
            n = jnp.where(t < CAUGHT_UP, 2 * (t - BASIS_FROM - BASIS_STEPS) + 1, t - LAG_GRID)
            synthesize(n)

            @pl.when(n > 1)
            def _():
                combine(n - 1, lax.rem(n - 1, 2))

        return carry

    lax.fori_loop(GROUPS, STEPS + LAG_RELAY, step, 0)

    last = STEPS - 1

    def last_sum(sources):
        rows = [pl.ds(pl.multiple_of(s * DEPTH, DEPTH), DEPTH) for s in sources]
        return matmul(
            jnp.concatenate([columns(last, s) for s in sources], axis=1),
            jnp.concatenate([basis[at, :] for at in rows], axis=0),
        )

    synthesize(last - 1)
    combine(last - 2, last % 2)
    to_up(last, 2, below).wait_recv()
    to_down(last, 1, above).wait_recv()
    partial[...] = last_sum([y, below, above])
    rows = TILE * TILE // 2
    block = basis[pl.ds(pl.multiple_of(across * DEPTH, DEPTH), DEPTH), :]
    for half, arrival in enumerate((fwd_up(last, across), fwd_down(last, across))):
        arrival.wait_recv()
        levels = slice(half * TILE // 2, (half + 1) * TILE // 2)
        at = slice(half * rows, (half + 1) * rows)
        values = partial[at] + matmul(whole[last, across, levels].reshape(rows, DEPTH), block)
        outgoing[last, levels] = values[:, LONS:].astype(BF16).reshape(TILE // 2, TILE, LONS)
        half_to_mate(half).start()
        kept[last % 2, at] = values[:, :LONS]
    combine(last - 1, (last - 1) % 2)
    combine(0, 2)
    half_to_mate(0).wait_recv()
    half_to_mate(1).wait_recv()
    settle(last, last % 2)

    for t in range(1, 2 * GROUPS):
        wait_all(t // GROUPS, t % GROUPS * 128, 128, a2a_send.at[t])
    for p in range(2, PIECES):
        wait_all(p, 0, LANES, a2a_send.at[2 * GROUPS - 2 + p])
    early_wait(early_send)
    early_up().wait_send()
    early_down().wait_send()
    early_fwd_up().wait_send()
    early_fwd_down().wait_send()

    def drain(t, carry):
        for part in (1, 2):
            to_up(t, part).wait_send()
            to_down(t, part).wait_send()
        fwd_up(t).wait_send()
        fwd_down(t).wait_send()
        return carry

    lax.fori_loop(1, STEPS, drain, 0)
    for t in range(STEPS - 1):
        to_mate(t).wait_send()
    for half in range(2):
        half_to_mate(half).wait_send()


def shards(spectral, legendre, slot_pairs):
    per_device = spectral.shape[0]
    dma = pltpu.SemaphoreType.DMA
    vmem = pltpu.VMEM
    return pl.pallas_call(
        kernel,
        out_shape=vmem((FLEV, BAND, LONS), BF16),
        in_specs=[pl.BlockSpec(memory_space=pltpu.HBM)] * 3,
        out_specs=pl.BlockSpec(memory_space=pltpu.VMEM),
        scratch_shapes=[
            pltpu.SMEM((PAIRS,), jnp.int32),
            vmem((PAIRS,), jnp.int32),
            vmem((per_device, HALF, M + 1), BF16),
            vmem((M + TILE, per_device, NORTH), BF16),
            vmem((per_device, M + TILE, NORTH), BF16),
            vmem((per_device, 2 * HALF, M + 1), BF16),
            vmem((per_device, 2 * HALF, NORTH), BF16),
            vmem((WAVES, PIECES, TILE, LANES), BF16),
            vmem((YS, WAVES, TILE, 128), BF16),
            vmem((WAVES, YS, TILE, 128), BF16),
            vmem((PIECES, WAVES, TILE, LANES), BF16),
            vmem((STEPS, YS, TILE, TILE, DEPTH), BF16),
            vmem((YS * DEPTH, 2 * LONS), BF16),
            vmem((512, 512), BF16),
            vmem((512, 512), BF16),
            vmem((3, TILE * TILE, LONS), F32),
            vmem((TILE * TILE, 2 * LONS), F32),
            vmem((STEPS, TILE, TILE, LONS), BF16),
            vmem((STEPS, TILE, TILE, LONS), BF16),
            dma((3,)), dma((CHUNKS + 1,)),
            dma((2 * GROUPS + PIECES - 2,)), dma((2 * GROUPS + PIECES - 2,)),
            dma, dma,
            dma((STEPS, 4)), dma((STEPS, 4)),
            dma((STEPS, 2)), dma((STEPS, 2)),
            dma((STEPS + 1,)), dma((STEPS + 1,)),
        ],
        compiler_params=pltpu.CompilerParams(
            collective_id=0, has_side_effects=True, vmem_limit_bytes=50 << 20
        ),
        name="spectral_to_grid",
    )(
        pltpu.with_memory_space_constraint(slot_pairs, pltpu.HBM),
        pltpu.with_memory_space_constraint(spectral.reshape(per_device, HALF, M + 1), pltpu.HBM),
        pltpu.with_memory_space_constraint(legendre.transpose(1, 0, 2), pltpu.HBM),
    )


def solution(mesh):
    in_specs = (P(("wave", "field"), None, None, None, None), P(("wave", "field"), None, None), P())
    out_specs = P(None, "wave", "field")
    return jax.shard_map(shards, mesh=mesh, in_specs=in_specs, out_specs=out_specs, check_vma=False)
```
